32 devices in a mesh: row: 8 (over z, x), col: 4 (over y, core).
Axes of the slice: x: 2, y: 2, z: 4, core: 2. Of those that a mesh axis runs over, the one named last changes fastest.
Arguments:
- eigen_vectors: float32 [8192, 2048], P('row', 'col'), may hold values from -6 to 6
- panel_first: float32 [8192, 512], P('row', 'col'), may hold values from -0.0625 to 0.0625
- panel_second: float32 [8192, 512], P('row', 'col'), may hold values from -0.0625 to 0.0625
- factor_first: float32 [512, 512], replicated, as said below
- factor_second: float32 [512, 512], replicated, as said below
Outputs:
- transformed: float32 [8192, 2048], P('row', 'col')
The draws below stay inside these ranges and needn't reach their ends.
Inputs may be any that keep to these rules, and one draw needn't show every extreme that they name: factor_first is upper triangular. factor_second is upper triangular.
All inputs are finite; a program needn't handle non-finite values.
Results may differ from the reference program's by a relative error of at most 0.0001.
Values sent between devices are 32-bit elements; how exact they have to be, the bound alone decides.
No kernel may reach another device: no remote copies, remote signals or barrier semaphores. Data moves between devices by JAX's collectives and lax.ppermute only.
A program may use at most 64 MiB of HBM per device.

```python
import math
import jax
import jax.numpy as jnp
from jax import lax

NB = 512
EIG = 2048
NROWS = 8192


def make_factor(key):
    values = jax.random.normal(key, (NB, NB), jnp.float32)
    upper_mask = jnp.triu(jnp.ones((NB, NB), jnp.float32))
    return values * upper_mask * (math.sqrt(2.0 * NROWS) / NB)


def draw_factor_first(key, part):
    return make_factor(jax.random.fold_in(key, 11))


def draw_factor_second(key, part):
    return make_factor(jax.random.fold_in(key, 23))


def steps_of(stream_key, dims, shards, low, high):
    factor_of = 1.0
    for dim, parts in shards:
        heights = jax.random.uniform(jax.random.fold_in(jax.random.fold_in(stream_key, 6), dim), (parts,), jnp.float32, low / len(shards), high / len(shards))
        factor_of = factor_of * jnp.repeat(jnp.exp(heights), dims[dim] // parts).reshape((-1,) + (1,) * (len(dims) - 1 - dim))
    return factor_of


def scatter_about(stream_key, extent, spread, most, split=(), held_as=jnp.bfloat16):
    array = jax.random.normal(stream_key, extent, jnp.float32) * spread
    if len(split) > 0:
        array = steps_of(stream_key, extent, split, -0.22, 0.18) * array
    return jnp.clip(array, min=-most, max=most).astype(held_as)


def setup_inputs(seed: int = 0) -> dict:
    keys = jax.random.split(jax.random.key(seed), 6)
    eigen_vectors = scatter_about(keys[0], (NROWS, EIG), 1.0, 6.0, ((0, 8), (1, 4)), jnp.float32)
    panel_first = scatter_about(keys[1], (NROWS, NB), NROWS ** -0.5, 0.0625, ((0, 8), (1, 4)), jnp.float32)
    panel_second = scatter_about(keys[2], (NROWS, NB), NROWS ** -0.5, 0.0625, ((0, 8), (1, 4)), jnp.float32)
    factor_first = draw_factor_first(jax.random.fold_in(keys[5], 71), 0)
    factor_second = draw_factor_second(jax.random.fold_in(keys[5], 71), 0)
    return dict(eigen_vectors=eigen_vectors, panel_first=panel_first, panel_second=panel_second, factor_first=factor_first, factor_second=factor_second)


def local_dot(left, right):
    return jnp.dot(left, right, precision=lax.Precision.HIGHEST, preferred_element_type=jnp.float32)


def reference(eigen_vectors, panel_first, panel_second, factor_first, factor_second):
    projected = local_dot(panel_second.T, eigen_vectors)
    after_second = eigen_vectors - local_dot(panel_second, local_dot(factor_second, projected))
    projected = local_dot(panel_first.T, after_second)
    return after_second - local_dot(panel_first, local_dot(factor_first, projected))
```

```python
import functools

import jax
import jax.numpy as jnp
from jax import lax
from jax.experimental import pallas as pl
from jax.experimental.pallas import tpu as pltpu
from jax.sharding import PartitionSpec as P

GROUP = 4
MIB = 1 << 20
NT = (((1,), (1,)), ((), ()))
NN = (((1,), (0,)), ((), ()))


def split(value):
    high = value.astype(jnp.bfloat16)
    return high, (value - high.astype(jnp.float32)).astype(jnp.bfloat16)


def dot3(left, right, dims):
    def one(a, b):
        return lax.dot_general(a, b, dims, preferred_element_type=jnp.float32)

    return one(left[0], right[1]) + one(left[1], right[0]) + one(left[0], right[0])


def joined(refs):
    return jnp.concatenate([ref[...] for ref in refs], axis=1)


def stacked(refs, cols=slice(None)):
    return jnp.concatenate([ref[:, cols] for ref in refs], axis=0)


def block(index, size):
    return pl.ds(pl.multiple_of(index * size, size), size)


def prepare_kernel(place, x, v, lt_high, lt_low, x_in, v_in, v_high, v_low, sems):
    wide, thin = x.shape[1] // GROUP, v.shape[1] // GROUP
    copies = [pltpu.make_async_copy(x.at[:, block(place[p], wide)], x_in.at[p], sems.at[p]) for p in range(GROUP)]
    copies.append(pltpu.make_async_copy(v, v_in, sems.at[GROUP]))
    for copy in copies:
        copy.start()
    for p in range(GROUP):
        copies[p].wait()
        high, rest = split(x_in[p])
        lt_high[p * wide : (p + 1) * wide, :] = high.T
        lt_low[p * wide : (p + 1) * wide, :] = rest.T
    copies[GROUP].wait()
    high, rest = split(v_in[...])
    v_high[...] = high.T
    v_low[...] = rest.T
    for p in range(GROUP):
        rows = slice(x.shape[1] + p * thin, x.shape[1] + (p + 1) * thin)
        lt_high[rows, :] = v_high[block(place[p], thin), :]
        lt_low[rows, :] = v_low[block(place[p], thin), :]


def arrange_kernel(width, place, t, t_high, t_low):
    col = place[GROUP]
    for i in range(t.shape[0] // width):
        for j in range(t.shape[0] // width):
            high, rest = split(t[block(col ^ i, width), block(col ^ j, width)])
            at = (slice(i * width, (i + 1) * width), slice(j * width, (j + 1) * width))
            t_high[at] = high
            t_low[at] = rest


def project_kernel(pairs, lt_high, lt_low, *refs):
    vectors, outs = refs[: 2 * pairs], refs[-2:]
    rows = outs[0].shape[0]
    left = (lt_high[: 2 * rows, :], lt_low[: 2 * rows, :])
    for k in range(pairs):
        total = dot3(left, split(joined(vectors[2 * k : 2 * k + 2])), NN)
        size = total.shape[1]
        for i in range(2):
            outs[i][:, k * size : (k + 1) * size] = total[i * rows : (i + 1) * rows, :]


def project_cross_kernel(lt_high, lt_low, near0, near1, far0, far1, *outs):
    thin = near0.shape[1] // GROUP
    cols = lt_high.shape[0] - GROUP * thin
    wide = cols // GROUP
    total = dot3((lt_high[...], lt_low[...]), split(joined((far0, far1))), NN)
    cross = dot3((lt_high[cols:, :], lt_low[cols:, :]), split(joined((near0, near1))), NN)
    for p in range(GROUP):
        out, at = outs[p // 2], (p % 2) * (wide + 2 * thin)
        out[at : at + wide, :] = total[p * wide : (p + 1) * wide, :]
        out[at + wide : at + wide + thin, :] = cross[p * thin : (p + 1) * thin, :]
        out[at + wide + thin : at + wide + 2 * thin, :] = total[cols + p * thin : cols + (p + 1) * thin, :]


def fold_kernel(keep, got, *refs):
    mine, other = refs[-2:]
    rows = mine.shape[0]
    mine[...] = keep[:rows, :] + got[:rows, :]
    other[...] = keep[rows:, :] + got[rows:, :]


def add_kernel(left, right, *refs):
    refs[-1][...] = left[...] + right[...]


def pile_kernel(count, *refs):
    parts, out = refs[:count], refs[-1]
    at = 0
    for part in parts:
        out[at : at + part.shape[0], :] = part[...]
        at += part.shape[0]


def cross_kernel(wide, place, low, high, out):
    width = out.shape[0] // 2
    half = out.shape[1] // 2
    thin = width // GROUP
    size = low.shape[0] // 2
    for i in range(2):
        for j in range(2):
            for p in range(GROUP):
                at = (p % 2) * size + wide + (2 * i + j) * thin
                to = pl.ds(pl.multiple_of(i * width + place[p] * thin, thin), thin)
                out[to, j * half : (j + 1) * half] = (low, high)[p // 2][at : at + thin, :]


def factor_kernel(t_high, t_low, v0, v1, v2, v3, w_high, w_low):
    tile = v0.shape[0] // 2
    right = (t_high[...], t_low[...])
    for i in range(2):
        at = slice(i * tile, (i + 1) * tile)
        left = split(jnp.concatenate([v[at, :] for v in (v0, v1, v2, v3)], axis=1))
        w_high[at, :], w_low[at, :] = split(dot3(left, right, NN))


def near_kernel(place, x, t_high, t_low, w_high, w_low, low, high, out, c):
    half = low.shape[1] // 2
    wide = low.shape[0] // 2
    p2 = split(stacked((low, high), slice(0, half)))
    c[...] = dot3(p2, (t_high[:, :half], t_low[:, :half]), NT)
    tile = x.shape[0] // 2
    for i in range(2):
        at = slice(i * tile, (i + 1) * tile)
        change = dot3((w_high[at, :half], w_low[at, :half]), p2, NT)
        for p in range(GROUP):
            cols = slice(p * wide, (p + 1) * wide)
            out[at, cols] = x[at, block(place[p], wide)] - change[:, cols]


def middle_kernel(x, t_high, t_low, w2_high, w2_low, w1_high, w1_low, c, g, g_core, n_low, n_high, low, high, out, rest):
    half = rest.shape[1]
    wide = n_low.shape[0] // 2
    width = g.shape[0] // 2
    size = low.shape[0] // 2
    p2 = split(
        jnp.concatenate([(low, high)[p // 2][(p % 2) * size : (p % 2) * size + wide, :] for p in range(GROUP)], axis=0)
    )
    c2 = split(c[...] + dot3(p2, (t_high[:, half:], t_low[:, half:]), NT))
    parts = []
    for i in range(4):
        rows = (g_core if i % 2 else g)[(i // 2) * width : (i // 2 + 1) * width, :]
        parts.append(jnp.concatenate([rows[:, (j ^ i) * width : ((j ^ i) + 1) * width] for j in range(4)], axis=1))
    cross = dot3(c2, split(jnp.concatenate(parts, axis=0)), NT)
    rest[...] = cross[:, half:]
    p1 = split(stacked((n_low, n_high), slice(half, 2 * half)) - cross[:, :half])
    tile = x.shape[0] // 2
    for i in range(2):
        at = slice(i * tile, (i + 1) * tile)
        change = dot3((w2_high[at, half:], w2_low[at, half:]), p2, NT)
        out[at, :] = x[at, :] - (change + dot3((w1_high[at, :half], w1_low[at, :half]), p1, NT))


def last_kernel(place, x, w_high, w_low, rest, low, high, out, tiles, sems):
    wide, half = low.shape[0] // 2, low.shape[1]
    right = split(stacked((low, high)) - rest[...])
    count = tiles.shape[0]
    tile = tiles.shape[1]
    copies = []
    for i in range(count):
        at = slice(i * tile, (i + 1) * tile)
        change = dot3((w_high[at, half:], w_low[at, half:]), right, NT)
        for p in range(GROUP):
            cols = slice(p * wide, (p + 1) * wide)
            tiles[i, :, block(place[p], wide)] = x[at, cols] - change[:, cols]
        copies.append(pltpu.make_async_copy(tiles.at[i], out.at[at, :], sems.at[i]))
        copies[i].start()
    for copy in copies:
        copy.wait()


def call(kernel, outs, operands, macs=0, scalars=0, scratch=(), out_space=pltpu.VMEM):
    specs = [pl.BlockSpec(memory_space=pltpu.SMEM)] * scalars
    values = []
    for value in operands[scalars:]:
        if isinstance(value, InAny):
            specs.append(pl.BlockSpec(memory_space=pl.ANY))
            values.append(value.array)
        elif isinstance(value, InHbm):
            specs.append(pl.BlockSpec(memory_space=pltpu.HBM))
            values.append(pltpu.with_memory_space_constraint(value.array, pltpu.HBM))
        else:
            specs.append(pl.BlockSpec(memory_space=pltpu.VMEM))
            values.append(value)
    return pl.pallas_call(
        kernel,
        out_shape=tuple(jax.ShapeDtypeStruct(shape, dtype) for shape, dtype in outs),
        in_specs=specs,
        out_specs=tuple(pl.BlockSpec(memory_space=out_space) for _ in outs),
        scratch_shapes=list(scratch),
        compiler_params=pltpu.CompilerParams(vmem_limit_bytes=36 * MIB),
        cost_estimate=pl.CostEstimate(flops=6 * macs, bytes_accessed=4096, transcendentals=0),
    )(*operands[:scalars], *values)


class InHbm:
    def __init__(self, array):
        self.array = array


class InAny:
    def __init__(self, array):
        self.array = array


def after(value, *earlier):
    return lax.optimization_barrier((value, earlier))[0]


def on_device(row_size, col_size, x, panel_first, panel_second, factor_first, factor_second):
    f32, bf16 = jnp.float32, jnp.bfloat16
    rows, cols = x.shape
    width = panel_first.shape[1]
    total = factor_first.shape[0]
    half = total // 2
    wide, thin = cols // GROUP, width // GROUP
    tall = cols + width
    col = lax.axis_index("col")
    low = lax.axis_index("row") % GROUP
    one, two = 1 + col % 2, 2 - col % 2
    place = jnp.stack([low, low ^ two, low ^ one, low ^ 3, col]).astype(jnp.int32)

    def permute(value, target):
        pairs = [
            (r * col_size + c, target(r, c)[0] * col_size + target(r, c)[1]) for r in range(row_size) for c in range(col_size)
        ]
        return lax.ppermute(value, ("row", "col"), pairs)

    def to_col(value, flip):
        return permute(value, lambda r, c: (r, c ^ flip))

    def to_one(value):
        return permute(value, lambda r, c: (r ^ (1 + c % 2), c))

    def to_two(value):
        return permute(value, lambda r, c: (r ^ (2 - c % 2), c))

    def add(left, right, *pads):
        return call(add_kernel, [(left.shape, f32)], (left, right, *map(InAny, pads)))[0]

    def across(value, *earlier, pads=()):
        bit = GROUP
        while bit < row_size:
            got = after(permute(value, lambda r, c, bit=bit: (r ^ bit, c)), *earlier)
            value = add(value, got, *pads)
            bit *= 2
        return value

    def pad(value):
        return to_col(value[:wide], 1)

    def fold(keep, sent, *pads):
        shape = (keep.shape[0] // 2, keep.shape[1])
        return call(fold_kernel, [(shape, f32)] * 2, (keep, to_one(sent), *map(InAny, pads)))

    def pile(*parts, pads=()):
        shape = (sum(p.shape[0] for p in parts), parts[0].shape[1])
        return call(functools.partial(pile_kernel, len(parts)), [(shape, f32)], (*parts, *map(InAny, pads)))[0]

    def spread(mine, *earlier):
        pair = pile(mine, after(to_two(mine), *earlier))
        return pair, to_one(pair)

    second_far = to_col(panel_second, 2)
    first_far = to_col(panel_first, 2)
    second_near = (panel_second, to_col(panel_second, 1))
    first_near = (panel_first, to_col(panel_first, 1))

    lt_high, lt_low = call(
        prepare_kernel,
        [((tall, rows), bf16)] * 2,
        (place, InHbm(x), InHbm(panel_first)),
        scalars=1,
        scratch=[
            pltpu.VMEM((GROUP, rows, wide), f32),
            pltpu.VMEM((rows, width), f32),
            pltpu.VMEM((width, rows), bf16),
            pltpu.VMEM((width, rows), bf16),
            pltpu.SemaphoreType.DMA((GROUP + 1,)),
        ],
    )
    near_parts = call(
        functools.partial(project_kernel, 2),
        [((2 * wide, total), f32)] * 2,
        (lt_high, lt_low, *second_near, *first_near),
    )
    second_far = after(second_far, near_parts)
    second_far = (second_far, to_col(second_far, 1))
    second = second_near + second_far
    near_mine, near_other = fold(*near_parts)
    near_sum = near_mine + to_two(near_other)
    second_parts = call(
        project_cross_kernel,
        [((2 * (wide + 2 * thin), half), f32)] * 2,
        (lt_high, lt_low, *second_near, after(second_far[0], near_other), second_far[1]),
    )
    second_mine, second_other = fold(second_parts[0], second_parts[1], pad(near_sum))
    second_sum = second_mine + to_two(second_other)

    near_sum = across(near_sum)
    first_far = after(first_far, second_other)
    first_far = (first_far, to_col(first_far, 1))
    first = first_near + first_far
    first_parts = call(
        functools.partial(project_kernel, 1),
        [((2 * wide, half), f32)] * 2,
        (lt_high, lt_low, *first_far),
    )
    second_sum = across(after(second_sum, near_sum))
    near = spread(near_sum)
    first_mine, first_other = fold(*first_parts)
    first_sum = first_mine + to_two(first_other)

    arrange = functools.partial(call, functools.partial(arrange_kernel, width), [((total, total), bf16)] * 2, scalars=1)
    factor = functools.partial(call, factor_kernel, [((rows, total), bf16)] * 2)
    t1 = arrange((place, factor_first), rows * total // 2)
    t2 = arrange((place, factor_second), rows * total // 2)
    w2 = factor((*t2, *second), rows * total * total)
    w1 = factor((*t1, *first), rows * total * total)
    left, coefficients = call(
        near_kernel,
        [((rows, cols), f32), ((cols, total), f32)],
        (place, x, *t2, *w2, *near),
        (rows + total) * cols * half,
        scalars=1,
    )

    second_sum = pile(second_sum, after(to_col(second_sum[wide:], 2), first_parts))
    second_blocks = spread(second_sum, w1, w2, first_other)
    first_sum = across(first_sum)
    (cross,) = call(
        functools.partial(cross_kernel, wide), [((2 * width, total), f32)], (place, *after(second_blocks, left, first_sum)), scalars=1
    )
    cross_core = to_col(cross, 1)
    first_blocks = spread(first_sum)

    left, rest = call(
        middle_kernel,
        [((rows, cols), f32), ((cols, half), f32)],
        (left, *t2, *w2, *w1, coefficients, cross, cross_core, *near, *second_blocks),
        (2 * rows + 2 * total) * cols * half,
    )
    tiles = 4
    (out,) = call(
        last_kernel,
        [((rows, cols), f32)],
        (place, left, *w1, rest, *first_blocks),
        rows * cols * half,
        scalars=1,
        scratch=[pltpu.VMEM((tiles, rows // tiles, cols), f32), pltpu.SemaphoreType.DMA((tiles,))],
        out_space=pl.ANY,
    )
    return out


def solution(mesh):
    return jax.shard_map(
        functools.partial(on_device, mesh.shape["row"], mesh.shape["col"]),
        mesh=mesh,
        in_specs=(P("row", "col"), P("row", "col"), P("row", "col"), P(), P()),
        out_specs=P("row", "col"),
        check_vma=False,
    )
```

```python
import functools

import jax
import jax.numpy as jnp
from jax import lax
from jax.experimental import pallas as pl
from jax.experimental.pallas import tpu as pltpu
from jax.sharding import PartitionSpec as P

GROUP = 4
MIB = 1 << 20
NT = (((1,), (1,)), ((), ()))
NN = (((1,), (0,)), ((), ()))


def split(value):
    high = value.astype(jnp.bfloat16)
    return high, (value - high.astype(jnp.float32)).astype(jnp.bfloat16)


def dot3(left, right, dims):
    def one(a, b):
        return lax.dot_general(a, b, dims, preferred_element_type=jnp.float32)

    return one(left[0], right[1]) + one(left[1], right[0]) + one(left[0], right[0])


def joined(refs):
    return jnp.concatenate([ref[...] for ref in refs], axis=1)


def stacked(refs, part=...):
    return jnp.concatenate([ref[part] for ref in refs], axis=0)


def block(index, size):
    return pl.ds(pl.multiple_of(index * size, size), size)


def prepare_kernel(place, x, v, lt_high, lt_low, x_in, v_in, v_high, v_low, sems):
    wide, thin = x.shape[1] // GROUP, v.shape[1] // GROUP
    copies = [pltpu.make_async_copy(x.at[:, block(place[p], wide)], x_in.at[p], sems.at[p]) for p in range(GROUP)]
    copies.append(pltpu.make_async_copy(v, v_in, sems.at[GROUP]))
    for copy in copies:
        copy.start()
    for p in range(GROUP):
        copies[p].wait()
        high, rest = split(x_in[p])
        lt_high[p * wide : (p + 1) * wide, :] = high.T
        lt_low[p * wide : (p + 1) * wide, :] = rest.T
    copies[GROUP].wait()
    high, rest = split(v_in[...])
    v_high[...] = high.T
    v_low[...] = rest.T
    for p in range(GROUP):
        rows = slice(x.shape[1] + p * thin, x.shape[1] + (p + 1) * thin)
        lt_high[rows, :] = v_high[block(place[p], thin), :]
        lt_low[rows, :] = v_low[block(place[p], thin), :]


def arrange_kernel(width, place, t, t_high, t_low):
    col = place[GROUP]
    for i in range(t.shape[0] // width):
        for j in range(t.shape[0] // width):
            high, rest = split(t[block(col ^ i, width), block(col ^ j, width)])
            at = (slice(i * width, (i + 1) * width), slice(j * width, (j + 1) * width))
            t_high[at] = high
            t_low[at] = rest


def put(total, at, *outs):
    rows = outs[0].shape[0]
    for p in range(GROUP):
        outs[p][:, at : at + total.shape[1]] = total[p * rows : (p + 1) * rows, :]


def project_kernel(lt_high, lt_low, *refs):
    vectors, outs = refs[:-GROUP], refs[-GROUP:]
    rows = GROUP * outs[0].shape[0]
    left = (lt_high[:rows, :], lt_low[:rows, :])
    for k in range(0, len(vectors), 2):
        total = dot3(left, split(joined(vectors[k : k + 2])), NN)
        put(total, k // 2 * total.shape[1], *outs)


def project_last_kernel(lt_high, lt_low, v0, *refs):
    pieces, outs = refs[:-GROUP], refs[-GROUP:]
    rows = GROUP * outs[0].shape[0]
    right = jnp.concatenate([v0[...], stacked(pieces)], axis=1)
    put(dot3((lt_high[:rows, :], lt_low[:rows, :]), split(right), NN), 0, *outs)


def project_cross_kernel(lt_high, lt_low, near0, near1, far0, *refs):
    thin = near0.shape[1] // GROUP
    cols = lt_high.shape[0] - GROUP * thin
    wide = cols // GROUP
    pieces, outs = refs[:-GROUP], refs[-GROUP:]
    far = jnp.concatenate([far0[...], stacked(pieces)], axis=1)
    total = dot3((lt_high[...], lt_low[...]), split(far), NN)
    cross = dot3((lt_high[cols:, :], lt_low[cols:, :]), split(joined((near0, near1))), NN)
    for p in range(GROUP):
        outs[p][:wide, :] = total[p * wide : (p + 1) * wide, :]
        outs[p][wide : wide + thin, :] = cross[p * thin : (p + 1) * thin, :]
        outs[p][wide + thin :, :] = total[cols + p * thin : cols + (p + 1) * thin, :]


def add_kernel(count, *refs):
    total = refs[0][...]
    for ref in refs[1:count]:
        total = total + ref[...]
    refs[-1][...] = total


def pile_kernel(count, *refs):
    parts, out = refs[:count], refs[-1]
    at = 0
    for part in parts:
        out[at : at + part.shape[0], :] = part[...]
        at += part.shape[0]


def cross_kernel(wide, place, *refs):
    blocks, out = refs[:GROUP], refs[GROUP]
    width = out.shape[0] // 2
    half = out.shape[1] // 2
    thin = width // GROUP
    for i in range(2):
        for j in range(2):
            at = wide + (2 * i + j) * thin
            for p in range(GROUP):
                to = pl.ds(pl.multiple_of(i * width + place[p] * thin, thin), thin)
                out[to, j * half : (j + 1) * half] = blocks[p][at : at + thin, :]


def factor_kernel(t_high, t_low, v0, v1, v2, *refs):
    pieces, (w_high, w_low) = refs[:-2], refs[-2:]
    count = 2
    tile = v0.shape[0] // count
    right = (t_high[...], t_low[...])
    for i in range(count):
        at = slice(i * tile, (i + 1) * tile)
        if len(pieces) == 1:
            last = pieces[0][at, :]
        else:
            each = len(pieces) // count
            last = jnp.concatenate([piece[...] for piece in pieces[i * each : (i + 1) * each]], axis=0)
        left = split(jnp.concatenate([v0[at, :], v1[at, :], v2[at, :], last], axis=1))
        w_high[at, :], w_low[at, :] = split(dot3(left, right, NN))


def near_kernel(place, x, t_high, t_low, w_high, w_low, *refs):
    blocks, (out, c) = refs[:GROUP], refs[GROUP:]
    wide, half = blocks[0].shape[0], blocks[0].shape[1] // 2
    p2 = split(stacked(blocks, (slice(None), slice(0, half))))
    c[...] = dot3(p2, (t_high[:, :half], t_low[:, :half]), NT)
    tile = x.shape[0] // 2
    for i in range(2):
        at = slice(i * tile, (i + 1) * tile)
        change = dot3((w_high[at, :half], w_low[at, :half]), p2, NT)
        for p in range(GROUP):
            cols = slice(p * wide, (p + 1) * wide)
            out[at, cols] = x[at, block(place[p], wide)] - change[:, cols]


def middle_kernel(x, t_high, t_low, w2_high, w2_low, w1_high, w1_low, c, g, g_core, *refs):
    near, far, (out, rest) = refs[:GROUP], refs[GROUP : 2 * GROUP], refs[2 * GROUP :]
    wide, half = near[0].shape[0], rest.shape[1]
    width = g.shape[0] // 2
    p2 = split(stacked(far, (slice(0, wide), slice(None))))
    c2 = split(c[...] + dot3(p2, (t_high[:, half:], t_low[:, half:]), NT))
    parts = []
    for i in range(4):
        rows = (g_core if i % 2 else g)[(i // 2) * width : (i // 2 + 1) * width, :]
        parts.append(jnp.concatenate([rows[:, (j ^ i) * width : ((j ^ i) + 1) * width] for j in range(4)], axis=1))
    cross = dot3(c2, split(jnp.concatenate(parts, axis=0)), NT)
    rest[...] = cross[:, half:]
    p1 = split(stacked(near, (slice(None), slice(half, 2 * half))) - cross[:, :half])
    tile = x.shape[0] // 2
    for i in range(2):
        at = slice(i * tile, (i + 1) * tile)
        change = dot3((w2_high[at, half:], w2_low[at, half:]), p2, NT)
        out[at, :] = x[at, :] - (change + dot3((w1_high[at, :half], w1_low[at, :half]), p1, NT))


def last_kernel(place, x, w_high, w_low, rest, b0, b1, b2, b3, out, tiles, sems):
    wide, half = b0.shape
    right = split(stacked((b0, b1, b2, b3)) - rest[...])
    count = tiles.shape[0]
    tile = tiles.shape[1]
    copies = []
    for i in range(count):
        at = slice(i * tile, (i + 1) * tile)
        change = dot3((w_high[at, half:], w_low[at, half:]), right, NT)
        for p in range(GROUP):
            cols = slice(p * wide, (p + 1) * wide)
            tiles[i, :, block(place[p], wide)] = x[at, cols] - change[:, cols]
        copies.append(pltpu.make_async_copy(tiles.at[i], out.at[at, :], sems.at[i]))
        copies[i].start()
    for copy in copies:
        copy.wait()


def call(kernel, outs, operands, macs=0, scalars=0, scratch=(), out_space=pltpu.VMEM):
    specs = [pl.BlockSpec(memory_space=pltpu.SMEM)] * scalars
    values = []
    for value in operands[scalars:]:
        if isinstance(value, InAny):
            specs.append(pl.BlockSpec(memory_space=pl.ANY))
            values.append(value.array)
        elif isinstance(value, InHbm):
            specs.append(pl.BlockSpec(memory_space=pltpu.HBM))
            values.append(pltpu.with_memory_space_constraint(value.array, pltpu.HBM))
        else:
            specs.append(pl.BlockSpec(memory_space=pltpu.VMEM))
            values.append(value)
    return pl.pallas_call(
        kernel,
        out_shape=tuple(jax.ShapeDtypeStruct(shape, dtype) for shape, dtype in outs),
        in_specs=specs,
        out_specs=tuple(pl.BlockSpec(memory_space=out_space) for _ in outs),
        scratch_shapes=list(scratch),
        compiler_params=pltpu.CompilerParams(vmem_limit_bytes=36 * MIB),
        cost_estimate=pl.CostEstimate(flops=6 * macs, bytes_accessed=4096, transcendentals=0),
    )(*operands[:scalars], *values)


class InHbm:
    def __init__(self, array):
        self.array = array


class InAny:
    def __init__(self, array):
        self.array = array


def after(value, *earlier):
    return lax.optimization_barrier((value, earlier))[0]


def on_device(row_size, col_size, x, panel_first, panel_second, factor_first, factor_second):
    f32, bf16 = jnp.float32, jnp.bfloat16
    rows, cols = x.shape
    width = panel_first.shape[1]
    total = factor_first.shape[0]
    half = total // 2
    wide, thin = cols // GROUP, width // GROUP
    tall = cols + width
    col = lax.axis_index("col")
    low = lax.axis_index("row") % GROUP
    one, two = 1 + col % 2, 2 - col % 2
    place = jnp.stack([low, low ^ two, low ^ one, low ^ 3, col]).astype(jnp.int32)

    def permute(value, target):
        pairs = [
            (r * col_size + c, target(r, c)[0] * col_size + target(r, c)[1]) for r in range(row_size) for c in range(col_size)
        ]
        return lax.ppermute(value, ("row", "col"), pairs)

    def to_col(value, flip):
        return permute(value, lambda r, c: (r, c ^ flip))

    def to_one(value):
        return permute(value, lambda r, c: (r ^ (1 + c % 2), c))

    def to_two(value):
        return permute(value, lambda r, c: (r ^ (2 - c % 2), c))

    def add(*parts, pads=()):
        return call(functools.partial(add_kernel, len(parts)), [(parts[0].shape, f32)], (*parts, *map(InAny, pads)))[0]

    def across(value, *earlier, pads=()):
        bit = GROUP
        while bit < row_size:
            got = after(permute(value, lambda r, c, bit=bit: (r ^ bit, c)), *earlier)
            value = add(value, got, pads=pads)
            bit *= 2
        return value

    def pad(value, rows=wide):
        return to_col(value[:rows], 1)

    def relayed(far):
        return far, *(to_col(piece, 1) for piece in jnp.split(far, 4))

    def projections(height, size):
        return [((height, size), f32)] * GROUP

    def pile(*parts, pads=()):
        shape = (sum(p.shape[0] for p in parts), parts[0].shape[1])
        return call(functools.partial(pile_kernel, len(parts)), [(shape, f32)], (*parts, *map(InAny, pads)))[0]

    def spread(mine, *earlier):
        got = to_two(mine)
        return mine, got, to_one(mine), to_one(after(got, *earlier))

    second_far = to_col(panel_second, 2)
    first_far = to_col(panel_first, 2)
    second_near = (panel_second, to_col(panel_second, 1))
    first_near = (panel_first, to_col(panel_first, 1))

    lt_high, lt_low = call(
        prepare_kernel,
        [((tall, rows), bf16)] * 2,
        (place, InHbm(x), InHbm(panel_first)),
        scalars=1,
        scratch=[
            pltpu.VMEM((GROUP, rows, wide), f32),
            pltpu.VMEM((rows, width), f32),
            pltpu.VMEM((width, rows), bf16),
            pltpu.VMEM((width, rows), bf16),
            pltpu.SemaphoreType.DMA((GROUP + 1,)),
        ],
    )
    near_parts = call(
        project_kernel, projections(wide, total), (lt_high, lt_low, *second_near, *first_near)
    )
    near_got = to_one(near_parts[2])
    near_other = add(near_parts[1], to_one(near_parts[3]), pads=(near_got,))

    second_far = relayed(after(second_far, near_other))
    second = second_near + second_far
    second_parts = call(
        project_cross_kernel,
        projections(wide + 2 * thin, half),
        (lt_high, lt_low, *second),
    )
    near_sum = add(near_parts[0], near_got, after(to_two(near_other), second_parts, first_far))
    second_got = to_one(second_parts[2])
    second_other = add(second_parts[1], to_one(second_parts[3]), pads=(second_got,))
    second_sum = add(second_parts[0], second_got, to_two(second_other))
    first_far = relayed(after(first_far, near_sum))
    first = first_near + first_far
    first_parts = call(project_last_kernel, projections(wide, half), (lt_high, lt_low, *first_far))
    arrange = functools.partial(call, functools.partial(arrange_kernel, width), [((total, total), bf16)] * 2, scalars=1)
    factor = functools.partial(call, factor_kernel, [((rows, total), bf16)] * 2)
    t1 = arrange((place, factor_first), rows * total // 2)
    t2 = arrange((place, factor_second), rows * total // 2)
    w2 = factor((*t2, *second), rows * total * total)
    w1 = factor((*t1, *first), rows * total * total)
    near_sum = across(near_sum, first_parts, w2)
    first_other = add(first_parts[1], to_one(first_parts[3]))
    first_sum = add(first_parts[0], to_one(first_parts[2]), to_two(first_other))
    second_sum = across(second_sum, first_other, pads=(pad(pad(near_sum), wide // 2),))
    near = spread(near_sum, first_other)

    left, coefficients = call(
        near_kernel,
        [((rows, cols), f32), ((cols, total), f32)],
        (place, x, *t2, *w2, *near),
        (rows + total) * cols * half,
        scalars=1,
    )

    second_sum = pile(second_sum, after(to_col(second_sum[wide:], 2), first_sum, w1))
    first_sum = across(first_sum)
    second_blocks = spread(second_sum, near)
    first_blocks = spread(first_sum)
    (cross,) = call(
        functools.partial(cross_kernel, wide),
        [((2 * width, total), f32)],
        (place, *after(second_blocks, left, first_blocks[1])),
        scalars=1,
    )
    cross_core = to_col(cross, 1)

    left, rest = call(
        middle_kernel,
        [((rows, cols), f32), ((cols, half), f32)],
        (left, *t2, *w2, *w1, coefficients, cross, cross_core, *near, *second_blocks),
        (2 * rows + 2 * total) * cols * half,
    )
    tiles = 4
    (out,) = call(
        last_kernel,
        [((rows, cols), f32)],
        (place, left, *w1, rest, *first_blocks),
        rows * cols * half,
        scalars=1,
        scratch=[pltpu.VMEM((tiles, rows // tiles, cols), f32), pltpu.SemaphoreType.DMA((tiles,))],
        out_space=pl.ANY,
    )
    return out


def solution(mesh):
    return jax.shard_map(
        functools.partial(on_device, mesh.shape["row"], mesh.shape["col"]),
        mesh=mesh,
        in_specs=(P("row", "col"), P("row", "col"), P("row", "col"), P(), P()),
        out_specs=P("row", "col"),
        check_vma=False,
    )
```

```python
import functools

import jax
import jax.numpy as jnp
from jax import lax
from jax.experimental import pallas as pl
from jax.experimental.pallas import tpu as pltpu
from jax.sharding import PartitionSpec as P

GROUP = 4
MIB = 1 << 20
NT = (((1,), (1,)), ((), ()))
NN = (((1,), (0,)), ((), ()))


def split(value):
    high = value.astype(jnp.bfloat16)
    return high, (value - high.astype(jnp.float32)).astype(jnp.bfloat16)


def dot3(left, right, dims):
    def one(a, b):
        return lax.dot_general(a, b, dims, preferred_element_type=jnp.float32)

    return one(left[0], right[1]) + one(left[1], right[0]) + one(left[0], right[0])


def joined(refs):
    return jnp.concatenate([ref[...] for ref in refs], axis=1)


def stacked(refs, part=...):
    return jnp.concatenate([ref[part] for ref in refs], axis=0)


def block(index, size):
    return pl.ds(pl.multiple_of(index * size, size), size)


def prepare_kernel(place, x, v, lt_high, lt_low, x_in, v_in, v_high, v_low, sems):
    wide, thin = x.shape[1] // GROUP, v.shape[1] // GROUP
    copies = [pltpu.make_async_copy(x.at[:, block(place[p], wide)], x_in.at[p], sems.at[p]) for p in range(GROUP)]
    copies.append(pltpu.make_async_copy(v, v_in, sems.at[GROUP]))
    for copy in copies:
        copy.start()
    for p in range(GROUP):
        copies[p].wait()
        high, rest = split(x_in[p])
        lt_high[p * wide : (p + 1) * wide, :] = high.T
        lt_low[p * wide : (p + 1) * wide, :] = rest.T
    copies[GROUP].wait()
    high, rest = split(v_in[...])
    v_high[...] = high.T
    v_low[...] = rest.T
    for p in range(GROUP):
        rows = slice(x.shape[1] + p * thin, x.shape[1] + (p + 1) * thin)
        lt_high[rows, :] = v_high[block(place[p], thin), :]
        lt_low[rows, :] = v_low[block(place[p], thin), :]


def arrange_kernel(width, place, t, t_high, t_low):
    col = place[GROUP]
    for i in range(t.shape[0] // width):
        for j in range(t.shape[0] // width):
            high, rest = split(t[block(col ^ i, width), block(col ^ j, width)])
            at = (slice(i * width, (i + 1) * width), slice(j * width, (j + 1) * width))
            t_high[at] = high
            t_low[at] = rest


def put(total, at, *outs):
    rows = outs[0].shape[0]
    for p in range(GROUP):
        outs[p][:, at : at + total.shape[1]] = total[p * rows : (p + 1) * rows, :]


def project_kernel(lt_high, lt_low, *refs):
    vectors, outs = refs[:-GROUP], refs[-GROUP:]
    rows = GROUP * outs[0].shape[0]
    left = (lt_high[:rows, :], lt_low[:rows, :])
    for k in range(0, len(vectors), 2):
        total = dot3(left, split(joined(vectors[k : k + 2])), NN)
        put(total, k // 2 * total.shape[1], *outs)


def project_last_kernel(lt_high, lt_low, v0, *refs):
    pieces, outs = refs[:-GROUP], refs[-GROUP:]
    rows = GROUP * outs[0].shape[0]
    right = jnp.concatenate([v0[...], stacked(pieces)], axis=1)
    put(dot3((lt_high[:rows, :], lt_low[:rows, :]), split(right), NN), 0, *outs)


def project_cross_kernel(lt_high, lt_low, near0, near1, far0, *refs):
    thin = near0.shape[1] // GROUP
    cols = lt_high.shape[0] - GROUP * thin
    wide = cols // GROUP
    pieces, outs = refs[:-GROUP], refs[-GROUP:]
    far = jnp.concatenate([far0[...], stacked(pieces)], axis=1)
    total = dot3((lt_high[...], lt_low[...]), split(far), NN)
    cross = dot3((lt_high[cols:, :], lt_low[cols:, :]), split(joined((near0, near1))), NN)
    for p in range(GROUP):
        outs[p][:wide, :] = total[p * wide : (p + 1) * wide, :]
        outs[p][wide : wide + thin, :] = cross[p * thin : (p + 1) * thin, :]
        outs[p][wide + thin :, :] = total[cols + p * thin : cols + (p + 1) * thin, :]


def add_kernel(count, *refs):
    total = refs[0][...]
    for ref in refs[1:count]:
        total = total + ref[...]
    refs[-1][...] = total


def pile_kernel(count, *refs):
    parts, out = refs[:count], refs[-1]
    at = 0
    for part in parts:
        out[at : at + part.shape[0], :] = part[...]
        at += part.shape[0]


def cross_kernel(wide, place, *refs):
    blocks, out = refs[:GROUP], refs[-1]
    width = out.shape[0] // 2
    half = out.shape[1] // 2
    thin = width // GROUP
    for i in range(2):
        for j in range(2):
            at = wide + (2 * i + j) * thin
            for p in range(GROUP):
                to = pl.ds(pl.multiple_of(i * width + place[p] * thin, thin), thin)
                out[to, j * half : (j + 1) * half] = blocks[p][at : at + thin, :]


def factor_kernel(t_high, t_low, v0, v1, v2, *refs):
    pieces, (w_high, w_low) = refs[:-2], refs[-2:]
    count = 2
    tile = v0.shape[0] // count
    right = (t_high[...], t_low[...])
    for i in range(count):
        at = slice(i * tile, (i + 1) * tile)
        if len(pieces) == 1:
            last = pieces[0][at, :]
        else:
            each = len(pieces) // count
            last = jnp.concatenate([piece[...] for piece in pieces[i * each : (i + 1) * each]], axis=0)
        left = split(jnp.concatenate([v0[at, :], v1[at, :], v2[at, :], last], axis=1))
        w_high[at, :], w_low[at, :] = split(dot3(left, right, NN))


def near_kernel(place, x, t_high, t_low, w_high, w_low, *refs):
    blocks, (out, c) = refs[:GROUP], refs[GROUP:]
    wide, half = blocks[0].shape[0], blocks[0].shape[1] // 2
    p2 = split(stacked(blocks, (slice(None), slice(0, half))))
    c[...] = dot3(p2, (t_high[:, :half], t_low[:, :half]), NT)
    tile = x.shape[0] // 2
    for i in range(2):
        at = slice(i * tile, (i + 1) * tile)
        change = dot3((w_high[at, :half], w_low[at, :half]), p2, NT)
        for p in range(GROUP):
            cols = slice(p * wide, (p + 1) * wide)
            out[at, cols] = x[at, block(place[p], wide)] - change[:, cols]


def middle_kernel(x, t_high, t_low, w2_high, w2_low, w1_high, w1_low, c, g, g_core, *refs):
    near, far, (out, rest) = refs[:GROUP], refs[GROUP : 2 * GROUP], refs[2 * GROUP :]
    wide, half = near[0].shape[0], rest.shape[1]
    width = g.shape[0] // 2
    p2 = split(stacked(far, (slice(0, wide), slice(None))))
    c2 = split(c[...] + dot3(p2, (t_high[:, half:], t_low[:, half:]), NT))
    parts = []
    for i in range(4):
        rows = (g_core if i % 2 else g)[(i // 2) * width : (i // 2 + 1) * width, :]
        parts.append(jnp.concatenate([rows[:, (j ^ i) * width : ((j ^ i) + 1) * width] for j in range(4)], axis=1))
    cross = dot3(c2, split(jnp.concatenate(parts, axis=0)), NT)
    rest[...] = cross[:, half:]
    p1 = split(stacked(near, (slice(None), slice(half, 2 * half))) - cross[:, :half])
    tile = x.shape[0] // 2
    for i in range(2):
        at = slice(i * tile, (i + 1) * tile)
        change = dot3((w2_high[at, half:], w2_low[at, half:]), p2, NT)
        out[at, :] = x[at, :] - (change + dot3((w1_high[at, :half], w1_low[at, :half]), p1, NT))


def last_kernel(place, x, w_high, w_low, rest, b0, b1, b2, b3, out, tiles, sems):
    wide, half = b0.shape
    right = split(stacked((b0, b1, b2, b3)) - rest[...])
    count = tiles.shape[0]
    tile = tiles.shape[1]
    copies = []
    for i in range(count):
        at = slice(i * tile, (i + 1) * tile)
        change = dot3((w_high[at, half:], w_low[at, half:]), right, NT)
        for p in range(GROUP):
            cols = slice(p * wide, (p + 1) * wide)
            tiles[i, :, block(place[p], wide)] = x[at, cols] - change[:, cols]
        copies.append(pltpu.make_async_copy(tiles.at[i], out.at[at, :], sems.at[i]))
        copies[i].start()
    for copy in copies:
        copy.wait()


def call(kernel, outs, operands, macs=0, scalars=0, scratch=(), out_space=pltpu.VMEM):
    specs = [pl.BlockSpec(memory_space=pltpu.SMEM)] * scalars
    values = []
    for value in operands[scalars:]:
        if isinstance(value, InAny):
            specs.append(pl.BlockSpec(memory_space=pl.ANY))
            values.append(value.array)
        elif isinstance(value, InHbm):
            specs.append(pl.BlockSpec(memory_space=pltpu.HBM))
            values.append(pltpu.with_memory_space_constraint(value.array, pltpu.HBM))
        else:
            specs.append(pl.BlockSpec(memory_space=pltpu.VMEM))
            values.append(value)
    return pl.pallas_call(
        kernel,
        out_shape=tuple(jax.ShapeDtypeStruct(shape, dtype) for shape, dtype in outs),
        in_specs=specs,
        out_specs=tuple(pl.BlockSpec(memory_space=out_space) for _ in outs),
        scratch_shapes=list(scratch),
        compiler_params=pltpu.CompilerParams(vmem_limit_bytes=36 * MIB),
        cost_estimate=pl.CostEstimate(flops=6 * macs, bytes_accessed=4096, transcendentals=0),
    )(*operands[:scalars], *values)


class InHbm:
    def __init__(self, array):
        self.array = array


class InAny:
    def __init__(self, array):
        self.array = array


def after(value, *earlier):
    return lax.optimization_barrier((value, earlier))[0]


def on_device(row_size, col_size, x, panel_first, panel_second, factor_first, factor_second):
    f32, bf16 = jnp.float32, jnp.bfloat16
    rows, cols = x.shape
    width = panel_first.shape[1]
    total = factor_first.shape[0]
    half = total // 2
    wide, thin = cols // GROUP, width // GROUP
    tall = cols + width
    col = lax.axis_index("col")
    low = lax.axis_index("row") % GROUP
    one, two = 1 + col % 2, 2 - col % 2
    place = jnp.stack([low, low ^ two, low ^ one, low ^ 3, col]).astype(jnp.int32)

    def permute(value, target):
        pairs = [
            (r * col_size + c, target(r, c)[0] * col_size + target(r, c)[1]) for r in range(row_size) for c in range(col_size)
        ]
        return lax.ppermute(value, ("row", "col"), pairs)

    def to_col(value, flip):
        return permute(value, lambda r, c: (r, c ^ flip))

    def to_one(value):
        return permute(value, lambda r, c: (r ^ (1 + c % 2), c))

    def to_two(value):
        return permute(value, lambda r, c: (r ^ (2 - c % 2), c))

    def add(*parts, pads=()):
        return call(functools.partial(add_kernel, len(parts)), [(parts[0].shape, f32)], (*parts, *map(InAny, pads)))[0]

    def across(value, *earlier, pads=()):
        bit = GROUP
        while bit < row_size:
            got = after(permute(value, lambda r, c, bit=bit: (r ^ bit, c)), *earlier)
            value = add(value, got, pads=pads)
            bit *= 2
        return value

    def pad(value, rows=wide):
        return to_col(value[:rows], 1)

    def relayed(far, pieces):
        return far, *(to_col(piece, 1) for piece in jnp.split(far, pieces))

    def projections(height, size):
        return [((height, size), f32)] * GROUP

    def pile(*parts, pads=()):
        shape = (sum(p.shape[0] for p in parts), parts[0].shape[1])
        return call(functools.partial(pile_kernel, len(parts)), [(shape, f32)], (*parts, *map(InAny, pads)))[0]

    def spread(mine, *earlier):
        got = to_two(mine)
        return mine, got, to_one(mine), to_one(after(got, *earlier))

    second_across = to_col(panel_second, 2)
    first_across = to_col(panel_first, 2)
    second_near = (panel_second, to_col(panel_second, 1))
    first_near = (panel_first, to_col(panel_first, 1))

    lt_high, lt_low = call(
        prepare_kernel,
        [((tall, rows), bf16)] * 2,
        (place, InHbm(x), InHbm(panel_first)),
        scalars=1,
        scratch=[
            pltpu.VMEM((GROUP, rows, wide), f32),
            pltpu.VMEM((rows, width), f32),
            pltpu.VMEM((width, rows), bf16),
            pltpu.VMEM((width, rows), bf16),
            pltpu.SemaphoreType.DMA((GROUP + 1,)),
        ],
    )
    near_parts = call(
        project_kernel, projections(wide, total), (lt_high, lt_low, *second_near, *first_near)
    )
    near_got = to_one(near_parts[2])
    near_other = add(near_parts[1], to_one(near_parts[3]), pads=(near_got,))
    second_far = relayed(after(second_across, near_other), 4)
    second = second_near + second_far
    second_parts = call(
        project_cross_kernel,
        projections(wide + 2 * thin, half),
        (lt_high, lt_low, *second),
    )
    near_sum = add(near_parts[0], near_got, after(to_two(near_other), second_parts))
    second_got = to_one(second_parts[2])
    second_other = add(second_parts[1], to_one(second_parts[3]), pads=(second_got,))
    second_sum = add(second_parts[0], second_got, to_two(second_other))
    first_far = relayed(after(first_across, near_sum), 4)
    first = first_near + first_far
    first_parts = call(project_last_kernel, projections(wide, half), (lt_high, lt_low, *first_far))
    arrange = functools.partial(call, functools.partial(arrange_kernel, width), [((total, total), bf16)] * 2, scalars=1)
    factor = functools.partial(call, factor_kernel, [((rows, total), bf16)] * 2)
    t1 = arrange((place, factor_first), rows * total // 2)
    t2 = arrange((place, factor_second), rows * total // 2)
    w2 = factor((*t2, *second), rows * total * total)
    w1 = factor((*t1, *first), rows * total * total)
    first_got = to_one(first_parts[2])
    first_other = add(first_parts[1], to_one(first_parts[3]), pads=(first_got,))
    first_sum = add(first_parts[0], first_got, after(to_two(first_other), second_sum))
    near_total = across(near_sum, first_parts, w2)
    second_total = across(after(second_sum, near_total), first_other, pads=(pad(pad(near_total), wide // 2),))
    near_two = to_two(near_total)
    near = (near_total, near_two, to_one(near_total), to_one(after(near_two, first_other)))
    left, coefficients = call(
        near_kernel,
        [((rows, cols), f32), ((cols, total), f32)],
        (place, x, *t2, *w2, *near),
        (rows + total) * cols * half,
        scalars=1,
    )
    second_packed = pile(second_total, after(to_col(second_total[wide:], 2), first_sum, w1))
    second_two = to_two(second_packed)
    first_total = across(after(first_sum, second_total))
    second_one = to_one(second_packed)
    second_last = to_one(after(second_two, near))
    second_blocks = (second_packed, second_two, second_one, second_last)
    first_two = to_two(first_total)
    first_one = to_one(first_total)
    first_blocks = (first_total, first_two, first_one, to_one(first_two))
    (cross,) = call(
        functools.partial(cross_kernel, wide),
        [((2 * width, total), f32)],
        (place, *after(second_blocks, left, first_two)),
        scalars=1,
    )
    cross_core = to_col(cross, 1)

    left, rest = call(
        middle_kernel,
        [((rows, cols), f32), ((cols, half), f32)],
        (left, *t2, *w2, *w1, coefficients, cross, cross_core, *near, *second_blocks),
        (2 * rows + 2 * total) * cols * half,
    )
    tiles = 4
    (out,) = call(
        last_kernel,
        [((rows, cols), f32)],
        (place, left, *w1, rest, *first_blocks),
        rows * cols * half,
        scalars=1,
        scratch=[pltpu.VMEM((tiles, rows // tiles, cols), f32), pltpu.SemaphoreType.DMA((tiles,))],
        out_space=pl.ANY,
    )
    return out


def solution(mesh):
    return jax.shard_map(
        functools.partial(on_device, mesh.shape["row"], mesh.shape["col"]),
        mesh=mesh,
        in_specs=(P("row", "col"), P("row", "col"), P("row", "col"), P(), P()),
        out_specs=P("row", "col"),
        check_vma=False,
    )
```

```python
import functools

import jax
import jax.numpy as jnp
from jax import lax
from jax.experimental import pallas as pl
from jax.experimental.pallas import tpu as pltpu
from jax.sharding import PartitionSpec as P

GROUP = 4
MIB = 1 << 20
NT = (((1,), (1,)), ((), ()))
NN = (((1,), (0,)), ((), ()))


def split(value):
    high = value.astype(jnp.bfloat16)
    return high, (value - high.astype(jnp.float32)).astype(jnp.bfloat16)


def dot3(left, right, dims):
    def one(a, b):
        return lax.dot_general(a, b, dims, preferred_element_type=jnp.float32)

    return one(left[0], right[1]) + one(left[1], right[0]) + one(left[0], right[0])


def joined(refs):
    return jnp.concatenate([ref[...] for ref in refs], axis=1)


def stacked(refs, part=...):
    return jnp.concatenate([ref[part] for ref in refs], axis=0)


def block(index, size):
    return pl.ds(pl.multiple_of(index * size, size), size)


def prepare_kernel(place, x, v, lt_high, lt_low, x_in, v_in, v_high, v_low, sems):
    wide, thin = x.shape[1] // GROUP, v.shape[1] // GROUP
    copies = [pltpu.make_async_copy(x.at[:, block(place[p], wide)], x_in.at[p], sems.at[p]) for p in range(GROUP)]
    copies.append(pltpu.make_async_copy(v, v_in, sems.at[GROUP]))
    for copy in copies:
        copy.start()
    for p in range(GROUP):
        copies[p].wait()
        high, rest = split(x_in[p])
        lt_high[p * wide : (p + 1) * wide, :] = high.T
        lt_low[p * wide : (p + 1) * wide, :] = rest.T
    copies[GROUP].wait()
    high, rest = split(v_in[...])
    v_high[...] = high.T
    v_low[...] = rest.T
    for p in range(GROUP):
        rows = slice(x.shape[1] + p * thin, x.shape[1] + (p + 1) * thin)
        lt_high[rows, :] = v_high[block(place[p], thin), :]
        lt_low[rows, :] = v_low[block(place[p], thin), :]


def arrange_kernel(width, place, t, t_high, t_low):
    col = place[GROUP]
    for i in range(t.shape[0] // width):
        for j in range(t.shape[0] // width):
            high, rest = split(t[block(col ^ i, width), block(col ^ j, width)])
            at = (slice(i * width, (i + 1) * width), slice(j * width, (j + 1) * width))
            t_high[at] = high
            t_low[at] = rest


def put(total, at, *outs):
    rows = outs[0].shape[0]
    for p in range(GROUP):
        outs[p][:, at : at + total.shape[1]] = total[p * rows : (p + 1) * rows, :]


def project_kernel(lt_high, lt_low, *refs):
    vectors, outs = refs[:-GROUP], refs[-GROUP:]
    rows = GROUP * outs[0].shape[0]
    left = (lt_high[:rows, :], lt_low[:rows, :])
    for k in range(0, len(vectors), 2):
        total = dot3(left, split(joined(vectors[k : k + 2])), NN)
        put(total, k // 2 * total.shape[1], *outs)


def project_last_kernel(lt_high, lt_low, v0, *refs):
    pieces, outs = refs[:-GROUP], refs[-GROUP:]
    rows = GROUP * outs[0].shape[0]
    right = jnp.concatenate([v0[...], stacked(pieces)], axis=1)
    put(dot3((lt_high[:rows, :], lt_low[:rows, :]), split(right), NN), 0, *outs)


def project_cross_kernel(lt_high, lt_low, near0, near1, far0, *refs):
    thin = near0.shape[1] // GROUP
    cols = lt_high.shape[0] - GROUP * thin
    wide = cols // GROUP
    pieces, outs = refs[:-GROUP], refs[-GROUP:]
    far = jnp.concatenate([far0[...], stacked(pieces)], axis=1)
    total = dot3((lt_high[...], lt_low[...]), split(far), NN)
    cross = dot3((lt_high[cols:, :], lt_low[cols:, :]), split(joined((near0, near1))), NN)
    for p in range(GROUP):
        outs[p][:wide, :] = total[p * wide : (p + 1) * wide, :]
        outs[p][wide : wide + thin, :] = cross[p * thin : (p + 1) * thin, :]
        outs[p][wide + thin :, :] = total[cols + p * thin : cols + (p + 1) * thin, :]


def add_kernel(count, *refs):
    total = refs[0][...]
    for ref in refs[1:count]:
        total = total + ref[...]
    refs[-1][...] = total


def pile_kernel(count, *refs):
    parts, out = refs[:count], refs[-1]
    at = 0
    for part in parts:
        out[at : at + part.shape[0], :] = part[...]
        at += part.shape[0]


def cross_kernel(wide, place, *refs):
    blocks, out = refs[:GROUP], refs[-1]
    width = out.shape[0] // 2
    half = out.shape[1] // 2
    thin = width // GROUP
    for i in range(2):
        for j in range(2):
            at = wide + (2 * i + j) * thin
            for p in range(GROUP):
                to = pl.ds(pl.multiple_of(i * width + place[p] * thin, thin), thin)
                out[to, j * half : (j + 1) * half] = blocks[p][at : at + thin, :]


def factor_kernel(t_high, t_low, v0, v1, v2, *refs):
    pieces, (w_high, w_low) = refs[:-2], refs[-2:]
    count = 2
    tile = v0.shape[0] // count
    right = (t_high[...], t_low[...])
    for i in range(count):
        at = slice(i * tile, (i + 1) * tile)
        if len(pieces) == 1:
            last = pieces[0][at, :]
        else:
            each = len(pieces) // count
            last = jnp.concatenate([piece[...] for piece in pieces[i * each : (i + 1) * each]], axis=0)
        left = split(jnp.concatenate([v0[at, :], v1[at, :], v2[at, :], last], axis=1))
        w_high[at, :], w_low[at, :] = split(dot3(left, right, NN))


def near_kernel(place, x, t_high, t_low, w_high, w_low, *refs):
    blocks, (out, c) = refs[:GROUP], refs[GROUP:]
    wide, half = blocks[0].shape[0], blocks[0].shape[1] // 2
    p2 = split(stacked(blocks, (slice(None), slice(0, half))))
    c[...] = dot3(p2, (t_high[:, :half], t_low[:, :half]), NT)
    tile = x.shape[0] // 2
    for i in range(2):
        at = slice(i * tile, (i + 1) * tile)
        change = dot3((w_high[at, :half], w_low[at, :half]), p2, NT)
        for p in range(GROUP):
            cols = slice(p * wide, (p + 1) * wide)
            out[at, cols] = x[at, block(place[p], wide)] - change[:, cols]


def middle_kernel(x, t_high, t_low, w2_high, w2_low, w1_high, w1_low, c, g, g_core, *refs):
    near, far, (out, rest) = refs[:GROUP], refs[GROUP : 2 * GROUP], refs[2 * GROUP :]
    wide, half = near[0].shape[0], rest.shape[1]
    width = g.shape[0] // 2
    p2 = split(stacked(far, (slice(0, wide), slice(None))))
    c2 = split(c[...] + dot3(p2, (t_high[:, half:], t_low[:, half:]), NT))
    parts = []
    for i in range(4):
        rows = (g_core if i % 2 else g)[(i // 2) * width : (i // 2 + 1) * width, :]
        parts.append(jnp.concatenate([rows[:, (j ^ i) * width : ((j ^ i) + 1) * width] for j in range(4)], axis=1))
    cross = dot3(c2, split(jnp.concatenate(parts, axis=0)), NT)
    rest[...] = cross[:, half:]
    p1 = split(stacked(near, (slice(None), slice(half, 2 * half))) - cross[:, :half])
    tile = x.shape[0] // 2
    for i in range(2):
        at = slice(i * tile, (i + 1) * tile)
        change = dot3((w2_high[at, half:], w2_low[at, half:]), p2, NT)
        out[at, :] = x[at, :] - (change + dot3((w1_high[at, :half], w1_low[at, :half]), p1, NT))


def last_kernel(place, x, w_high, w_low, rest, b0, b1, b2, b3, out, tiles, sems):
    wide, half = b0.shape
    right = split(stacked((b0, b1, b2, b3)) - rest[...])
    count = tiles.shape[0]
    tile = tiles.shape[1]
    copies = []
    for i in range(count):
        at = slice(i * tile, (i + 1) * tile)
        change = dot3((w_high[at, half:], w_low[at, half:]), right, NT)
        for p in range(GROUP):
            cols = slice(p * wide, (p + 1) * wide)
            tiles[i, :, block(place[p], wide)] = x[at, cols] - change[:, cols]
        copies.append(pltpu.make_async_copy(tiles.at[i], out.at[at, :], sems.at[i]))
        copies[i].start()
    for copy in copies:
        copy.wait()


def call(kernel, outs, operands, macs=0, scalars=0, scratch=(), out_space=pltpu.VMEM):
    specs = [pl.BlockSpec(memory_space=pltpu.SMEM)] * scalars
    values = []
    for value in operands[scalars:]:
        if isinstance(value, InAny):
            specs.append(pl.BlockSpec(memory_space=pl.ANY))
            values.append(value.array)
        elif isinstance(value, InHbm):
            specs.append(pl.BlockSpec(memory_space=pltpu.HBM))
            values.append(pltpu.with_memory_space_constraint(value.array, pltpu.HBM))
        else:
            specs.append(pl.BlockSpec(memory_space=pltpu.VMEM))
            values.append(value)
    return pl.pallas_call(
        kernel,
        out_shape=tuple(jax.ShapeDtypeStruct(shape, dtype) for shape, dtype in outs),
        in_specs=specs,
        out_specs=tuple(pl.BlockSpec(memory_space=out_space) for _ in outs),
        scratch_shapes=list(scratch),
        compiler_params=pltpu.CompilerParams(vmem_limit_bytes=36 * MIB),
        cost_estimate=pl.CostEstimate(flops=6 * macs, bytes_accessed=4096, transcendentals=0),
    )(*operands[:scalars], *values)


class InHbm:
    def __init__(self, array):
        self.array = array


class InAny:
    def __init__(self, array):
        self.array = array


def after(value, *earlier):
    return lax.optimization_barrier((value, earlier))[0]


def on_device(row_size, col_size, x, panel_first, panel_second, factor_first, factor_second):
    f32, bf16 = jnp.float32, jnp.bfloat16
    rows, cols = x.shape
    width = panel_first.shape[1]
    total = factor_first.shape[0]
    half = total // 2
    wide, thin = cols // GROUP, width // GROUP
    tall = cols + width
    col = lax.axis_index("col")
    low = lax.axis_index("row") % GROUP
    one, two = 1 + col % 2, 2 - col % 2
    place = jnp.stack([low, low ^ two, low ^ one, low ^ 3, col]).astype(jnp.int32)

    def permute(value, target):
        pairs = [
            (r * col_size + c, target(r, c)[0] * col_size + target(r, c)[1]) for r in range(row_size) for c in range(col_size)
        ]
        return lax.ppermute(value, ("row", "col"), pairs)

    def to_col(value, flip):
        return permute(value, lambda r, c: (r, c ^ flip))

    def to_one(value):
        return permute(value, lambda r, c: (r ^ (1 + c % 2), c))

    def to_two(value):
        return permute(value, lambda r, c: (r ^ (2 - c % 2), c))

    def add(*parts, pads=()):
        return call(functools.partial(add_kernel, len(parts)), [(parts[0].shape, f32)], (*parts, *map(InAny, pads)))[0]

    def across(value, *earlier, pads=()):
        bit = GROUP
        while bit < row_size:
            got = after(permute(value, lambda r, c, bit=bit: (r ^ bit, c)), *earlier)
            value = add(value, got, pads=pads)
            bit *= 2
        return value

    def pad(value, rows=wide):
        return to_col(value[:rows], 1)

    def relayed(far, pieces):
        return far, *(to_col(piece, 1) for piece in jnp.split(far, pieces))

    def projections(height, size):
        return [((height, size), f32)] * GROUP

    def pile(*parts, pads=()):
        shape = (sum(p.shape[0] for p in parts), parts[0].shape[1])
        return call(functools.partial(pile_kernel, len(parts)), [(shape, f32)], (*parts, *map(InAny, pads)))[0]

    def spread(mine, *earlier):
        got = to_two(mine)
        return mine, got, to_one(mine), to_one(after(got, *earlier))

    second_across = to_col(panel_second, 2)
    first_across = to_col(panel_first, 2)
    second_near = (panel_second, to_col(panel_second, 1))
    first_near = (panel_first, to_col(panel_first, 1))

    lt_high, lt_low = call(
        prepare_kernel,
        [((tall, rows), bf16)] * 2,
        (place, InHbm(x), InHbm(panel_first)),
        scalars=1,
        scratch=[
            pltpu.VMEM((GROUP, rows, wide), f32),
            pltpu.VMEM((rows, width), f32),
            pltpu.VMEM((width, rows), bf16),
            pltpu.VMEM((width, rows), bf16),
            pltpu.SemaphoreType.DMA((GROUP + 1,)),
        ],
    )
    near_parts = call(
        project_kernel, projections(wide, total), (lt_high, lt_low, *second_near, *first_near)
    )
    near_got = to_one(near_parts[2])
    near_other = add(near_parts[1], to_one(near_parts[3]), pads=(near_got,))
    second_far = relayed(after(second_across, near_other), 4)
    second = second_near + second_far
    second_parts = call(
        project_cross_kernel,
        projections(wide + 2 * thin, half),
        (lt_high, lt_low, *second),
    )
    near_sum = add(near_parts[0], near_got, after(to_two(near_other), second_parts))
    second_got = to_one(second_parts[2])
    second_other = add(second_parts[1], to_one(second_parts[3]), pads=(second_got,))
    second_sum = add(second_parts[0], second_got, to_two(second_other))
    first_far = relayed(after(first_across, near_sum), 4)
    first = first_near + first_far
    first_parts = call(project_last_kernel, projections(wide, half), (lt_high, lt_low, *first_far))
    arrange = functools.partial(call, functools.partial(arrange_kernel, width), [((total, total), bf16)] * 2, scalars=1)
    factor = functools.partial(call, factor_kernel, [((rows, total), bf16)] * 2)
    t1 = arrange((place, factor_first), rows * total // 2)
    t2 = arrange((place, factor_second), rows * total // 2)
    w2 = factor((*after(t2, second_other), *second), rows * total * total)
    w1 = factor((*t1, *first), rows * total * total)
    first_got = to_one(first_parts[2])
    first_other = add(first_parts[1], to_one(first_parts[3]), pads=(first_got,))
    first_sum = add(first_parts[0], first_got, after(to_two(first_other), second_sum))
    near_total = across(near_sum, first_parts, w2)
    second_total = across(after(second_sum, near_total), first_other, pads=(pad(pad(near_total), wide // 2),))
    near_two = to_two(near_total)
    near = (near_total, near_two, to_one(near_total), to_one(after(near_two, first_other)))
    left, coefficients = call(
        near_kernel,
        [((rows, cols), f32), ((cols, total), f32)],
        (place, x, *t2, *w2, *near),
        (rows + total) * cols * half,
        scalars=1,
    )
    second_packed = pile(second_total, after(to_col(second_total[wide:], 2), first_sum, w1))
    second_two = to_two(second_packed)
    first_total = across(after(first_sum, second_total))
    second_one = to_one(second_packed)
    second_last = to_one(after(second_two, near))
    second_blocks = (second_packed, second_two, second_one, second_last)
    first_two = to_two(first_total)
    first_one = to_one(first_total)
    first_blocks = (first_total, first_two, first_one, to_one(first_two))
    (cross,) = call(
        functools.partial(cross_kernel, wide),
        [((2 * width, total), f32)],
        (place, *after(second_blocks, left, first_two)),
        scalars=1,
    )
    cross_core = to_col(cross, 1)

    left, rest = call(
        middle_kernel,
        [((rows, cols), f32), ((cols, half), f32)],
        (left, *t2, *w2, *w1, coefficients, cross, cross_core, *near, *second_blocks),
        (2 * rows + 2 * total) * cols * half,
    )
    tiles = 4
    (out,) = call(
        last_kernel,
        [((rows, cols), f32)],
        (place, left, *w1, rest, *first_blocks),
        rows * cols * half,
        scalars=1,
        scratch=[pltpu.VMEM((tiles, rows // tiles, cols), f32), pltpu.SemaphoreType.DMA((tiles,))],
        out_space=pl.ANY,
    )
    return out


def solution(mesh):
    return jax.shard_map(
        functools.partial(on_device, mesh.shape["row"], mesh.shape["col"]),
        mesh=mesh,
        in_specs=(P("row", "col"), P("row", "col"), P("row", "col"), P(), P()),
        out_specs=P("row", "col"),
        check_vma=False,
    )
```

```python
import functools

import jax
import jax.numpy as jnp
from jax import lax
from jax.experimental import pallas as pl
from jax.experimental.pallas import tpu as pltpu
from jax.sharding import PartitionSpec as P

GROUP = 4
MIB = 1 << 20
NT = (((1,), (1,)), ((), ()))
NN = (((1,), (0,)), ((), ()))


def split(value):
    high = value.astype(jnp.bfloat16)
    return high, (value - high.astype(jnp.float32)).astype(jnp.bfloat16)


def dot3(left, right, dims):
    def one(a, b):
        return lax.dot_general(a, b, dims, preferred_element_type=jnp.float32)

    return one(left[0], right[1]) + one(left[1], right[0]) + one(left[0], right[0])


def joined(refs):
    return jnp.concatenate([ref[...] for ref in refs], axis=1)


def stacked(refs, part=...):
    return jnp.concatenate([ref[part] for ref in refs], axis=0)


def block(index, size):
    return pl.ds(pl.multiple_of(index * size, size), size)


def prepare_kernel(place, x, v, lt_high, lt_low, x_in, v_in, v_high, v_low, sems):
    wide, thin = x.shape[1] // GROUP, v.shape[1] // GROUP
    copies = [pltpu.make_async_copy(x.at[:, block(place[p], wide)], x_in.at[p], sems.at[p]) for p in range(GROUP)]
    copies.append(pltpu.make_async_copy(v, v_in, sems.at[GROUP]))
    for copy in copies:
        copy.start()
    for p in range(GROUP):
        copies[p].wait()
        high, rest = split(x_in[p])
        lt_high[p * wide : (p + 1) * wide, :] = high.T
        lt_low[p * wide : (p + 1) * wide, :] = rest.T
    copies[GROUP].wait()
    high, rest = split(v_in[...])
    v_high[...] = high.T
    v_low[...] = rest.T
    for p in range(GROUP):
        rows = slice(x.shape[1] + p * thin, x.shape[1] + (p + 1) * thin)
        lt_high[rows, :] = v_high[block(place[p], thin), :]
        lt_low[rows, :] = v_low[block(place[p], thin), :]


def arrange_kernel(width, place, t, t_high, t_low):
    col = place[GROUP]
    for i in range(t.shape[0] // width):
        for j in range(t.shape[0] // width):
            high, rest = split(t[block(col ^ i, width), block(col ^ j, width)])
            at = (slice(i * width, (i + 1) * width), slice(j * width, (j + 1) * width))
            t_high[at] = high
            t_low[at] = rest


def put(total, at, *outs):
    rows = outs[0].shape[0]
    for p in range(GROUP):
        outs[p][:, at : at + total.shape[1]] = total[p * rows : (p + 1) * rows, :]


def project_kernel(lt_high, lt_low, *refs):
    vectors, outs = refs[:-GROUP], refs[-GROUP:]
    rows = GROUP * outs[0].shape[0]
    left = (lt_high[:rows, :], lt_low[:rows, :])
    for k in range(0, len(vectors), 2):
        total = dot3(left, split(joined(vectors[k : k + 2])), NN)
        put(total, k // 2 * total.shape[1], *outs)


def project_last_kernel(lt_high, lt_low, v0, *refs):
    pieces, outs = refs[:-GROUP], refs[-GROUP:]
    rows = GROUP * outs[0].shape[0]
    right = jnp.concatenate([v0[...], stacked(pieces)], axis=1)
    put(dot3((lt_high[:rows, :], lt_low[:rows, :]), split(right), NN), 0, *outs)


def project_cross_kernel(lt_high, lt_low, near0, near1, far0, *refs):
    thin = near0.shape[1] // GROUP
    cols = lt_high.shape[0] - GROUP * thin
    wide = cols // GROUP
    pieces, outs = refs[:-GROUP], refs[-GROUP:]
    far = jnp.concatenate([far0[...], stacked(pieces)], axis=1)
    total = dot3((lt_high[...], lt_low[...]), split(far), NN)
    cross = dot3((lt_high[cols:, :], lt_low[cols:, :]), split(joined((near0, near1))), NN)
    for p in range(GROUP):
        outs[p][:wide, :] = total[p * wide : (p + 1) * wide, :]
        outs[p][wide : wide + thin, :] = cross[p * thin : (p + 1) * thin, :]
        outs[p][wide + thin :, :] = total[cols + p * thin : cols + (p + 1) * thin, :]


def add_kernel(count, *refs):
    total = refs[0][...]
    for ref in refs[1:count]:
        total = total + ref[...]
    refs[-1][...] = total


def pile_kernel(count, *refs):
    parts, out = refs[:count], refs[-1]
    at = 0
    for part in parts:
        out[at : at + part.shape[0], :] = part[...]
        at += part.shape[0]


def cross_kernel(wide, place, *refs):
    blocks, out = refs[:GROUP], refs[-1]
    width = out.shape[0] // 2
    half = out.shape[1] // 2
    thin = width // GROUP
    for i in range(2):
        for j in range(2):
            at = wide + (2 * i + j) * thin
            for p in range(GROUP):
                to = pl.ds(pl.multiple_of(i * width + place[p] * thin, thin), thin)
                out[to, j * half : (j + 1) * half] = blocks[p][at : at + thin, :]


def factor_kernel(t_high, t_low, v0, v1, v2, *refs):
    pieces, (w_high, w_low) = refs[:-2], refs[-2:]
    count = 2
    tile = v0.shape[0] // count
    right = (t_high[...], t_low[...])
    for i in range(count):
        at = slice(i * tile, (i + 1) * tile)
        if len(pieces) == 1:
            last = pieces[0][at, :]
        else:
            each = len(pieces) // count
            last = jnp.concatenate([piece[...] for piece in pieces[i * each : (i + 1) * each]], axis=0)
        left = split(jnp.concatenate([v0[at, :], v1[at, :], v2[at, :], last], axis=1))
        w_high[at, :], w_low[at, :] = split(dot3(left, right, NN))


def near_kernel(place, x, t_high, t_low, w_high, w_low, *refs):
    blocks, (out, c) = refs[:GROUP], refs[GROUP:]
    wide, half = blocks[0].shape[0], blocks[0].shape[1] // 2
    p2 = split(stacked(blocks, (slice(None), slice(0, half))))
    c[...] = dot3(p2, (t_high[:, :half], t_low[:, :half]), NT)
    tile = x.shape[0] // 2
    for i in range(2):
        at = slice(i * tile, (i + 1) * tile)
        change = dot3((w_high[at, :half], w_low[at, :half]), p2, NT)
        for p in range(GROUP):
            cols = slice(p * wide, (p + 1) * wide)
            out[at, cols] = x[at, block(place[p], wide)] - change[:, cols]


def middle_kernel(x, t_high, t_low, w2_high, w2_low, w1_high, w1_low, c, g, g_core, *refs):
    near, far, (out, rest) = refs[:GROUP], refs[GROUP : 2 * GROUP], refs[2 * GROUP :]
    wide, half = near[0].shape[0], rest.shape[1]
    width = g.shape[0] // 2
    p2 = split(stacked(far, (slice(0, wide), slice(None))))
    c2 = split(c[...] + dot3(p2, (t_high[:, half:], t_low[:, half:]), NT))
    parts = []
    for i in range(4):
        rows = (g_core if i % 2 else g)[(i // 2) * width : (i // 2 + 1) * width, :]
        parts.append(jnp.concatenate([rows[:, (j ^ i) * width : ((j ^ i) + 1) * width] for j in range(4)], axis=1))
    cross = dot3(c2, split(jnp.concatenate(parts, axis=0)), NT)
    rest[...] = cross[:, half:]
    p1 = split(stacked(near, (slice(None), slice(half, 2 * half))) - cross[:, :half])
    tile = x.shape[0] // 2
    for i in range(2):
        at = slice(i * tile, (i + 1) * tile)
        change = dot3((w2_high[at, half:], w2_low[at, half:]), p2, NT)
        out[at, :] = x[at, :] - (change + dot3((w1_high[at, :half], w1_low[at, :half]), p1, NT))


def last_kernel(place, x, w_high, w_low, rest, b0, b1, b2, b3, out, tiles, sems):
    wide, half = b0.shape
    right = split(stacked((b0, b1, b2, b3)) - rest[...])
    count = tiles.shape[0]
    tile = tiles.shape[1]
    copies = []
    for i in range(count):
        at = slice(i * tile, (i + 1) * tile)
        change = dot3((w_high[at, half:], w_low[at, half:]), right, NT)
        for p in range(GROUP):
            cols = slice(p * wide, (p + 1) * wide)
            tiles[i, :, block(place[p], wide)] = x[at, cols] - change[:, cols]
        copies.append(pltpu.make_async_copy(tiles.at[i], out.at[at, :], sems.at[i]))
        copies[i].start()
    for copy in copies:
        copy.wait()


def call(kernel, outs, operands, macs=0, scalars=0, scratch=(), out_space=pltpu.VMEM):
    specs = [pl.BlockSpec(memory_space=pltpu.SMEM)] * scalars
    values = []
    for value in operands[scalars:]:
        if isinstance(value, InAny):
            specs.append(pl.BlockSpec(memory_space=pl.ANY))
            values.append(value.array)
        elif isinstance(value, InHbm):
            specs.append(pl.BlockSpec(memory_space=pltpu.HBM))
            values.append(pltpu.with_memory_space_constraint(value.array, pltpu.HBM))
        else:
            specs.append(pl.BlockSpec(memory_space=pltpu.VMEM))
            values.append(value)
    return pl.pallas_call(
        kernel,
        out_shape=tuple(jax.ShapeDtypeStruct(shape, dtype) for shape, dtype in outs),
        in_specs=specs,
        out_specs=tuple(pl.BlockSpec(memory_space=out_space) for _ in outs),
        scratch_shapes=list(scratch),
        compiler_params=pltpu.CompilerParams(vmem_limit_bytes=36 * MIB),
        cost_estimate=pl.CostEstimate(flops=6 * macs, bytes_accessed=4096, transcendentals=0),
    )(*operands[:scalars], *values)


class InHbm:
    def __init__(self, array):
        self.array = array


class InAny:
    def __init__(self, array):
        self.array = array


def after(value, *earlier):
    return lax.optimization_barrier((value, earlier))[0]


def on_device(row_size, col_size, x, panel_first, panel_second, factor_first, factor_second):
    f32, bf16 = jnp.float32, jnp.bfloat16
    rows, cols = x.shape
    width = panel_first.shape[1]
    total = factor_first.shape[0]
    half = total // 2
    wide, thin = cols // GROUP, width // GROUP
    tall = cols + width
    col = lax.axis_index("col")
    low = lax.axis_index("row") % GROUP
    one, two = 1 + col % 2, 2 - col % 2
    place = jnp.stack([low, low ^ two, low ^ one, low ^ 3, col]).astype(jnp.int32)

    def permute(value, target):
        pairs = [
            (r * col_size + c, target(r, c)[0] * col_size + target(r, c)[1]) for r in range(row_size) for c in range(col_size)
        ]
        return lax.ppermute(value, ("row", "col"), pairs)

    def to_col(value, flip):
        return permute(value, lambda r, c: (r, c ^ flip))

    def to_one(value):
        return permute(value, lambda r, c: (r ^ (1 + c % 2), c))

    def to_two(value):
        return permute(value, lambda r, c: (r ^ (2 - c % 2), c))

    def add(*parts, pads=()):
        return call(functools.partial(add_kernel, len(parts)), [(parts[0].shape, f32)], (*parts, *map(InAny, pads)))[0]

    def across(value, *earlier, pads=()):
        bit = GROUP
        while bit < row_size:
            got = after(permute(value, lambda r, c, bit=bit: (r ^ bit, c)), *earlier)
            value = add(value, got, pads=pads)
            bit *= 2
        return value

    def pad(value, rows=wide):
        return to_col(value[:rows], 1)

    def relayed(far, pieces):
        return far, *(to_col(piece, 1) for piece in jnp.split(far, pieces))

    def projections(height, size):
        return [((height, size), f32)] * GROUP

    def pile(*parts, pads=()):
        shape = (sum(p.shape[0] for p in parts), parts[0].shape[1])
        return call(functools.partial(pile_kernel, len(parts)), [(shape, f32)], (*parts, *map(InAny, pads)))[0]

    def spread(mine, *earlier):
        got = to_two(mine)
        return mine, got, to_one(mine), to_one(after(got, *earlier))

    second_across = to_col(panel_second, 2)
    first_across = to_col(panel_first, 2)
    second_near = (panel_second, to_col(panel_second, 1))
    first_near = (panel_first, to_col(panel_first, 1))

    lt_high, lt_low = call(
        prepare_kernel,
        [((tall, rows), bf16)] * 2,
        (place, InHbm(x), InHbm(panel_first)),
        scalars=1,
        scratch=[
            pltpu.VMEM((GROUP, rows, wide), f32),
            pltpu.VMEM((rows, width), f32),
            pltpu.VMEM((width, rows), bf16),
            pltpu.VMEM((width, rows), bf16),
            pltpu.SemaphoreType.DMA((GROUP + 1,)),
        ],
    )
    near_parts = call(
        project_kernel, projections(wide, total), (lt_high, lt_low, *second_near, *first_near)
    )
    near_got = to_one(near_parts[2])
    near_other = add(near_parts[1], to_one(near_parts[3]), pads=(near_got,))
    second_far = relayed(after(second_across, near_other), 4)
    second = second_near + second_far
    second_parts = call(
        project_cross_kernel,
        projections(wide + 2 * thin, half),
        (lt_high, lt_low, *second),
    )
    near_sum = add(near_parts[0], near_got, after(to_two(near_other), second_parts))
    second_got = to_one(second_parts[2])
    second_other = add(second_parts[1], to_one(second_parts[3]), pads=(second_got,))
    second_sum = add(second_parts[0], second_got, to_two(second_other))
    first_far = relayed(after(first_across, near_sum), 4)
    first = first_near + first_far
    first_parts = call(project_last_kernel, projections(wide, half), (lt_high, lt_low, *first_far))
    arrange = functools.partial(call, functools.partial(arrange_kernel, width), [((total, total), bf16)] * 2, scalars=1)
    factor = functools.partial(call, factor_kernel, [((rows, total), bf16)] * 2)
    t1 = arrange((place, factor_first), rows * total // 2)
    t2 = arrange((place, factor_second), rows * total // 2)
    w2 = factor((*t2, *second), rows * total * total)
    w1 = factor((*t1, *first), rows * total * total)
    first_got = to_one(first_parts[2])
    first_other = add(first_parts[1], to_one(first_parts[3]), pads=(first_got,))
    first_sum = add(first_parts[0], first_got, after(to_two(first_other), second_sum))
    near_total = across(near_sum, first_parts, w2)
    near_two = to_two(near_total)
    near_one = to_one(after(near_total, first_sum))
    second_total = across(after(second_sum, near_total), first_other, pads=(pad(pad(near_total), wide // 2),))
    near = (near_total, near_two, near_one, to_one(after(near_two, first_other)))
    left, coefficients = call(
        near_kernel,
        [((rows, cols), f32), ((cols, total), f32)],
        (place, x, *t2, *w2, *near),
        int(0.0 * (rows + total) * cols * half),
        scalars=1,
    )
    second_packed = pile(second_total, after(to_col(second_total[wide:], 2), first_sum, w1))
    second_two = to_two(second_packed)
    first_total = across(after(first_sum, second_total))
    second_one = to_one(second_packed)
    second_last = to_one(after(second_two, near))
    second_blocks = (second_packed, second_two, second_one, second_last)
    first_two = to_two(first_total)
    first_one = to_one(first_total)
    first_blocks = (first_total, first_two, first_one, to_one(first_two))
    (cross,) = call(
        functools.partial(cross_kernel, wide),
        [((2 * width, total), f32)],
        (place, *after(second_blocks, left, first_two)),
        scalars=1,
    )
    cross_core = to_col(cross, 1)

    left, rest = call(
        middle_kernel,
        [((rows, cols), f32), ((cols, half), f32)],
        (left, *t2, *w2, *w1, coefficients, cross, cross_core, *near, *second_blocks),
        (2 * rows + 2 * total) * cols * half,
    )
    tiles = 4
    (out,) = call(
        last_kernel,
        [((rows, cols), f32)],
        (place, left, *w1, rest, *first_blocks),
        rows * cols * half,
        scalars=1,
        scratch=[pltpu.VMEM((tiles, rows // tiles, cols), f32), pltpu.SemaphoreType.DMA((tiles,))],
        out_space=pl.ANY,
    )
    return out


def solution(mesh):
    return jax.shard_map(
        functools.partial(on_device, mesh.shape["row"], mesh.shape["col"]),
        mesh=mesh,
        in_specs=(P("row", "col"), P("row", "col"), P("row", "col"), P(), P()),
        out_specs=P("row", "col"),
        check_vma=False,
    )
```
